128 devices in a mesh: node: 16 (over z, x_lo, core), dev: 8 (over y, x_hi).
Axes of the slice: x: 4 (x_hi: 2, x_lo: 2; x = x_hi * 2 + x_lo), y: 4, z: 4, core: 2. Of those that a mesh axis runs over, the one named last changes fastest.
Arguments:
- hidden: bfloat16 [64, 7168], P('node'), may hold values from -6 to 6
- queries: bfloat16 [64, 128, 576], P('node'), may hold values from -8 to 8
- latent_cache: bfloat16 [64, 16384, 576], P('node', 'dev'), may hold values from -10 to 10
- lengths: int32 [64], P('node'), may hold values from 1 to 16384, 524288 in all
- value_up: bfloat16 [128, 512, 128], P(('node', 'dev')), may hold values from -6 to 6
- output_weight: bfloat16 [16384, 7168], P(('node', 'dev')), may hold values from -0.046875 to 0.046875
- norm_gain: float32 [7168], replicated, may hold values from 0.25 to 1.75
- routes: int32 [64, 8], P('node'), may hold values from 0 to 15, all different within a row; in each aligned block of 4 rows (0 to 3, 4 to 7, ...) at most 3 rows name the same one
- route_scores: float32 [64, 8], P('node'), may hold values from 0.05 to 1
- gate_weight: bfloat16 [16, 7168, 2048], P('node', None, 'dev'), may hold values from -0.0625 to 0.0625
- up_weight: bfloat16 [16, 7168, 2048], P('node', None, 'dev'), may hold values from -0.0625 to 0.0625
- down_weight: bfloat16 [16, 2048, 7168], P('node', 'dev'), may hold values from -0.125 to 0.125
Outputs:
- layer_out: float32 [64, 7168], P('node', 'dev')
The draws below stay inside these ranges and needn't reach their ends.
Inputs may be any that keep to these rules, and one draw needn't show every extreme that they name: `routes`: each row names 8 different experts; among the rows of one index of node no expert is named by more than 3 rows, and in every draw some expert reaches 3.
All inputs are finite; a program needn't handle non-finite values. No bound on the sum of `lengths` on one device may be relied on, other than what follows from the above.
Results may differ from the reference program's by a relative error of at most 0.0095.
Values may be sent and summed in bfloat16 or wider, within the bound.
No kernel may reach another device: no remote copies, remote signals or barrier semaphores. Data moves between devices by JAX's collectives and lax.ppermute only.
A program may use at most 128 MiB of HBM per device.

```python
import math
import jax
import jax.numpy as jnp
import numpy as np
from jax import lax

D = 7168
HEADS = 128
LAT = 512
ROPE = 64
VDIM = 128
FF = 2048
TOPK = 8
ROWS_NODE = 4
EXPERTS = 16
ROWS = 64
LEN = 16384
CAP = 3


def draw_latent_cache(key, part):
    key = jax.random.fold_in(key, 3)
    noise_key = jax.random.fold_in(key, 0)
    noise = jnp.clip(jax.random.normal(noise_key, (ROWS, LEN, LAT + ROPE), jnp.float32), -4.0, 4.0)
    return noise.astype(jnp.bfloat16)


def draw_queries(key, part):
    key = jax.random.fold_in(key, 5)
    noise_key = jax.random.fold_in(key, 0)
    noise = jnp.clip(jax.random.normal(noise_key, (ROWS, HEADS, LAT + ROPE), jnp.float32), -4.0, 4.0)
    return noise.astype(jnp.bfloat16)


def levels(key, shape, shards, low, top_value):
    def one(dim, blocks):
        steps = jax.random.uniform(jax.random.fold_in(jax.random.fold_in(key, 6), dim), (blocks,), jnp.float32, low / len(shards), top_value / len(shards))
        return jnp.repeat(jnp.exp(steps), shape[dim] // blocks).reshape((-1,) + (1,) * (len(shape) - dim - 1))

    factor_of = one(*shards[0])
    for cut in shards[1:]:
        factor_of = factor_of * one(*cut)
    return factor_of


def length_profile(amount, total, bound, skew):
    loads = [(1 << 20) // math.isqrt(rank ** skew) + 1 for rank in range(2, amount + 1)]
    rest, counts = total - bound - (amount - 1), [1] * (amount - 1)
    while rest > 0:
        candidates = [i for i in range(amount - 1) if counts[i] < bound]
        mass, remaining = sum([loads[i] for i in candidates]), rest
        for i in candidates:
            more = min(bound - counts[i], max(1, remaining * loads[i] // mass), rest)
            counts[i] = counts[i] + more
            rest = rest - more
    return np.array([bound] + counts)


def uneven(stream_key, count, total, reach, skew):
    if count == 2:
        one = jax.random.randint(stream_key, (), max(1, total - reach), min(reach, total - 1) + 1)
        return jnp.stack([one, total - one])
    sizes = jnp.asarray(length_profile(count, total, reach, skew), jnp.int32)
    pairs = (count - 1) // 2
    donor, receiver = sizes[1:1 + 2 * pairs:2], sizes[2:2 + 2 * pairs:2]
    margin = jnp.minimum(donor - 1, reach - receiver)
    moved = jax.random.randint(jax.random.fold_in(stream_key, 1), (pairs,), 0, 1 << 20) % (margin + 1)
    sizes = sizes.at[1:1 + 2 * pairs:2].set(donor - moved).at[2:2 + 2 * pairs:2].set(receiver + moved)
    return sizes[jax.random.permutation(jax.random.fold_in(stream_key, 2), count)]


def deal_out(own_key, own, number, rows, count, top, most, lean):
    ranking = jax.random.permutation(own_key, count)
    crowded, ordinary = shares(count, rows * top, most, lean, True), shares(count, rows * top, most, lean, False)
    places = jnp.arange(count)

    def named(sizes, rotation):
        used = int((sizes > 0).sum())
        fixed = max(1, used // 4)
        passed = fixed + (places - fixed + rotation * (used - fixed)) % max(1, count - fixed)
        return jnp.zeros((count,), jnp.int32).at[ranking[jnp.where(places < fixed, places, passed)]].set(jnp.asarray(sizes, jnp.int32))

    sizes = jnp.where(number % 4 == 0, named(crowded, number // 4), named(ordinary, number - number // 4 - 1))
    mixed = jax.random.permutation(jax.random.fold_in(own, 3), count)
    source_of, taker = mixed[0:count // 2 * 2:2], mixed[1:count // 2 * 2:2]
    slack = jnp.minimum(sizes[source_of] - 1, most - sizes[taker]) // 2
    slack = jnp.where((source_of == ranking[0]) | (taker == ranking[0]) | (sizes[taker] == 0), 0, jnp.maximum(slack, 0))
    passed = jax.random.randint(jax.random.fold_in(own, 4), (count // 2,), 0, 1 << 20) % (slack + 1)
    sizes = sizes.at[source_of].add(-passed).at[taker].add(passed)
    members = jnp.searchsorted(jnp.cumsum(sizes), jnp.arange(rows * top), side="right").astype(jnp.int32)
    grid = members.reshape(top, rows).T
    grid = grid[jax.random.permutation(jax.random.fold_in(own, 1), rows)]
    rotation = jax.random.randint(jax.random.fold_in(own, 2), (rows, 1), 0, top)
    return jnp.take_along_axis(grid, (jnp.arange(top)[None, :] + rotation) % top, axis=1)


def shares(number_of, total, reach, slope, full):
    loads = [(1 << 20) // math.isqrt(grade ** slope) + 1 for grade in range(1, number_of + 1)]
    largest = reach if full else min(reach, max(-(-total // number_of), total * loads[0] // sum(loads)))
    least = 1 if total - largest >= number_of - 1 else 0
    given, surplus = [largest] + [least] * (number_of - 1), total - largest - least * (number_of - 1)
    while surplus > 0:
        free = [i for i in range(1, number_of) if given[i] < largest] or [i for i in range(1, number_of) if given[i] < reach]
        whole, budget = sum([loads[i] for i in free]), surplus
        for i in free:
            addition = min(reach - given[i], max(1, budget * loads[i] // whole), surplus)
            given[i] = given[i] + addition
            surplus = surplus - addition
    return np.array(given)


def bell_draw(own_key, shape, scale, limit, shards=(), kind=jnp.bfloat16):
    gain = levels(own_key, shape, shards, -0.22, 0.18) if shards else 1.0
    values = jax.random.normal(own_key, shape, jnp.float32) * scale * gain
    return jnp.minimum(jnp.maximum(values, -limit), limit).astype(kind)


def setup_inputs(seed: int = 0) -> dict:
    streams_of = jax.random.split(jax.random.key(seed), 13)
    hidden = bell_draw(streams_of[0], (ROWS, D), 1.0, 6.0, ((0, 16),))
    queries = draw_queries(jax.random.fold_in(streams_of[12], 71), 0)
    latent_cache = draw_latent_cache(jax.random.fold_in(streams_of[12], 71), 0)
    lengths = uneven(streams_of[3], ROWS, ROWS * LEN // 2, LEN, 2).astype(jnp.int32)
    value_up = bell_draw(streams_of[4], (HEADS, LAT, VDIM), 1.0, 6.0, ((0, 128),))
    output_weight = bell_draw(streams_of[5], (HEADS * VDIM, D), (HEADS * VDIM) ** -0.5, 0.046875, ((0, 128),))
    norm_gain = jnp.clip(1.0 + 0.15 * jax.random.normal(streams_of[6], (D,), jnp.float32), 0.25, 1.75)
    routes_keys = jax.random.split(jax.random.fold_in(streams_of[7], 1), ROWS // ROWS_NODE)
    routes_turns = jax.random.permutation(jax.random.fold_in(streams_of[7], 3), ROWS // ROWS_NODE)
    routes = jax.vmap(lambda own, number: deal_out(jax.random.fold_in(streams_of[7], 2), own, number, ROWS_NODE, EXPERTS, TOPK, CAP, 2))(routes_keys, routes_turns).reshape((ROWS, TOPK))
    route_scores = jnp.clip(jnp.exp(math.log(1.0) - 2.9957323 * jax.random.uniform(streams_of[8], (ROWS, TOPK), jnp.float32) ** levels(streams_of[8], (ROWS, TOPK), ((0, 16),), -0.2, 0.2)), 0.05, 1.0)
    gate_weight = bell_draw(streams_of[9], (EXPERTS, D, FF), D ** -0.5, 0.0625, ((0, 16), (2, 8)))
    up_weight = bell_draw(streams_of[10], (EXPERTS, D, FF), D ** -0.5, 0.0625, ((0, 16), (2, 8)))
    down_weight = bell_draw(streams_of[11], (EXPERTS, FF, D), FF ** -0.5, 0.125, ((0, 16), (1, 8)))
    return {"hidden": hidden, "queries": queries, "latent_cache": latent_cache, "lengths": lengths, "value_up": value_up, "output_weight": output_weight, "norm_gain": norm_gain, "routes": routes, "route_scores": route_scores, "gate_weight": gate_weight, "up_weight": up_weight, "down_weight": down_weight}


def attend_row(packed):
    query_row, cache_rows, row_length = packed
    scaling = (LAT + ROPE) ** (-0.5)
    scores = jnp.dot(query_row, cache_rows.T, preferred_element_type=jnp.float32) * scaling
    is_valid = jnp.arange(LEN) < row_length
    masked = jnp.where(is_valid[None, :], scores, -1e+30)
    row_max = lax.optimization_barrier(jnp.max(masked, axis=1, keepdims=True))
    weights = jnp.where(is_valid[None, :], jnp.exp(masked - row_max), 0.0)
    row_total = lax.optimization_barrier(jnp.sum(weights, axis=1, keepdims=True))
    summed = jnp.dot(weights.astype(jnp.bfloat16), cache_rows[:, :LAT], preferred_element_type=jnp.float32)
    return (summed / row_total).astype(jnp.bfloat16)

def reference(hidden, queries, latent_cache, lengths, value_up, output_weight, norm_gain, routes, route_scores, gate_weight, up_weight, down_weight):
    attended = lax.map(attend_row, (queries, latent_cache, lengths))
    head_values = jnp.einsum('rhl,hlv->rhv', attended.astype(jnp.float32), value_up.astype(jnp.float32))
    head_values = head_values.astype(jnp.bfloat16).reshape(ROWS, HEADS * VDIM)
    attention_out = jnp.dot(head_values, output_weight, preferred_element_type=jnp.float32)
    residual_float = hidden.astype(jnp.float32) + attention_out
    mean_square = lax.optimization_barrier(jnp.mean(residual_float * residual_float, axis=1, keepdims=True))
    normed = (residual_float * lax.rsqrt(mean_square + 1e-06) * norm_gain).astype(jnp.bfloat16)
    mix_weights = 2.5 * route_scores / lax.optimization_barrier(jnp.sum(route_scores, axis=1, keepdims=True))

    def expert_step(combined, expert_index):
        gate_part = jnp.dot(normed, gate_weight[expert_index], preferred_element_type=jnp.float32)
        up_part = jnp.dot(normed, up_weight[expert_index], preferred_element_type=jnp.float32)
        activated = (jax.nn.silu(gate_part) * up_part).astype(jnp.bfloat16)
        expert_out = jnp.dot(activated, down_weight[expert_index], preferred_element_type=jnp.float32).astype(jnp.bfloat16)
        coefficient = lax.optimization_barrier(jnp.sum(jnp.where(routes == expert_index, mix_weights, 0.0), axis=1))
        return (combined + coefficient[:, None] * expert_out.astype(jnp.float32), None)
    combined, _ = lax.scan(expert_step, jnp.zeros((ROWS, D), jnp.float32), jnp.arange(EXPERTS, dtype=jnp.int32))
    return residual_float + combined
```

```python
import functools

import jax
import jax.numpy as jnp
from jax import lax
from jax.experimental import pallas as pl
from jax.experimental.pallas import tpu as pltpu
from jax.sharding import Mesh
from jax.sharding import PartitionSpec as P

PLANE = ("pair", "dev")
VMEM = pl.BlockSpec(memory_space=pltpu.VMEM)
SMEM = pl.BlockSpec(memory_space=pltpu.SMEM)
ANY = pl.BlockSpec(memory_space=pl.ANY)
NOTES = 128
LIMIT = 40 * 2**20
f32 = jnp.float32
bf16 = jnp.bfloat16


def exchange(blocks):
    return lax.all_to_all(blocks, PLANE, split_axis=0, concat_axis=0, tiled=True)


def other_core(value):
    return lax.ppermute(value, "core", [(0, 1), (1, 0)])


def thirds(value):
    high = value.astype(bf16).astype(f32)
    rest = value - high
    middle = rest.astype(bf16).astype(f32)
    return high, middle, rest - middle


def attend_kernel(
    lengths, routes, route_scores, query, cache, out, held, joined, arrivals
):
    rows, feature, positions = cache.shape
    heads = query.shape[2]
    tiles = joined.shape[0] - 1
    latent = tiles * NOTES
    dev = lax.axis_index("dev")
    dev_count = lax.axis_size("dev")
    copies = [
        pltpu.make_async_copy(cache.at[row], held.at[row], arrivals.at[row]) for row in range(rows)
    ]
    for copy in copies:
        copy.start()
    lane = lax.broadcasted_iota(jnp.int32, (heads, NOTES), 1)
    expert = lax.broadcasted_iota(jnp.int32, (heads, NOTES), 0) // dev_count
    position = lax.broadcasted_iota(jnp.int32, (heads, positions), 1)
    scale = feature**-0.5
    for row in range(rows):
        used = lengths[row] - dev * positions
        total_score = route_scores[row, 0]
        for k in range(1, routes.shape[1]):
            total_score = total_score + route_scores[row, k]
        named = jnp.zeros((heads, NOTES), f32)
        for k in range(routes.shape[1]):
            named = jnp.where(expert == routes[row, k], route_scores[row, k], named)
        coefficient = 2.5 * named / total_score
        copies[row].wait()
        scores = lax.dot_general(
            query[row], held[row], (((0,), (0,)), ((), ())), preferred_element_type=f32
        )
        scores = jnp.where(position < used, scores, -1e30)
        top = jnp.max(scores, axis=1, keepdims=True)
        weights = jnp.exp((scores - top) * scale)
        total = jnp.sum(weights, axis=1, keepdims=True)
        summed = lax.dot_general(
            weights.astype(bf16),
            held[row, :latent, :],
            (((1,), (1,)), ((), ())),
            preferred_element_type=f32,
        )
        mean = summed / total
        log_total = jnp.where(used > 0, top * scale + jnp.log(total), -1e30)
        notes = jnp.zeros((heads, NOTES), f32)
        for place, part in enumerate(thirds(log_total) + thirds(coefficient)):
            notes = jnp.where(lane == place, part, notes)
        for group in range(heads // 8):
            pair, core = group // 2, group % 2
            target = pl.ds(pair * 64 + core * rows + row, 8, stride=8)
            source = slice(group * 8, group * 8 + 8)
            for tile in range(tiles):
                joined[tile, target] = mean[source, tile * NOTES : (tile + 1) * NOTES]
            joined[tiles, target] = notes[source]
    for tile in range(tiles + 1):
        columns = slice(tile * NOTES, (tile + 1) * NOTES)
        out[:, :, columns] = joined[tile].astype(bf16).reshape(out.shape[0], out.shape[1], NOTES)


def attend(lengths, routes, route_scores, queries, cache, latent):
    rows, feature, positions = cache.shape
    heads = queries.shape[2]
    return pl.pallas_call(
        attend_kernel,
        out_shape=jax.ShapeDtypeStruct((heads // 2, 2 * rows, latent + NOTES), bf16),
        in_specs=[SMEM, SMEM, SMEM, VMEM, ANY],
        out_specs=VMEM,
        scratch_shapes=[
            pltpu.VMEM((rows, feature, positions), bf16),
            pltpu.VMEM((latent // NOTES + 1, heads * rows, NOTES), f32),
            pltpu.SemaphoreType.DMA((rows,)),
        ],
        compiler_params=pltpu.CompilerParams(vmem_limit_bytes=LIMIT),
        cost_estimate=pl.CostEstimate(
            flops=4 * rows * heads * feature * positions,
            bytes_accessed=2 * rows * feature * positions,
            transcendentals=rows * heads * positions,
        ),
        name="attend",
    )(lengths, routes, route_scores, queries, cache)


def project_kernel(arrived, up_own, up_other, out_own, out_other, part, coefficients):
    pairs, devs, rows, share = part.shape
    latent = up_own.shape[0]
    core = lax.axis_index("core")
    notes = arrived[:, :, latent:].astype(f32)
    lane = lax.broadcasted_iota(jnp.int32, notes.shape, 2)
    log_total = jnp.sum(jnp.where(lane < 3, notes, 0.0), axis=2, keepdims=True)
    coefficient = jnp.sum(
        jnp.where((lane >= 3) & (lane < 6), notes, 0.0), axis=2, keepdims=True
    )
    coefficient = coefficient.reshape(pairs, devs, 2 * rows, 1)[:, 0]
    coefficient = jnp.broadcast_to(coefficient, (pairs, 2 * rows, NOTES))
    coefficients[0] = coefficient[:, :rows]
    coefficients[1] = coefficient[:, rows:]
    log_total = log_total.reshape(pairs, devs, 2 * rows, 1)
    weight = jnp.exp(log_total - jnp.max(log_total, axis=1, keepdims=True))
    weight = weight / jnp.sum(weight, axis=1, keepdims=True)
    values = arrived[:, :, :latent].reshape(pairs, devs, 2 * rows, latent)
    attended = weight[:, 0] * values[:, 0].astype(f32)
    for dev in range(1, devs):
        attended = attended + weight[:, dev] * values[:, dev].astype(f32)
    attended = attended.reshape(pairs * 2 * rows, latent).astype(bf16)

    def head(up, is_own):
        value = jnp.dot(attended, up[...], preferred_element_type=f32)
        value = value.reshape(pairs, 2 * rows, -1)
        low, high = value[:, :rows], value[:, rows:]
        picked = jnp.where(core == (0 if is_own else 1), low, high)
        return picked.reshape(pairs * rows, -1).astype(bf16)

    own, other = head(up_own, True), head(up_other, False)
    for dev in range(devs):
        columns = slice(dev * share, (dev + 1) * share)
        value = jnp.dot(own, out_own[:, columns], preferred_element_type=f32)
        value = value + jnp.dot(other, out_other[:, columns], preferred_element_type=f32)
        part[:, dev] = value.astype(bf16).reshape(pairs, rows, share)


def project(arrived, up_own, up_other, out_own, out_other, pairs, devs):
    rows = arrived.shape[1] // 2
    width = out_own.shape[1]
    return pl.pallas_call(
        project_kernel,
        out_shape=(
            jax.ShapeDtypeStruct((pairs, devs, rows, width // devs), bf16),
            jax.ShapeDtypeStruct((2, pairs, rows, NOTES), f32),
        ),
        in_specs=[VMEM] * 5,
        out_specs=(VMEM, VMEM),
        compiler_params=pltpu.CompilerParams(vmem_limit_bytes=LIMIT),
        name="project",
    )(arrived, up_own, up_other, out_own, out_other)


def residual_kernel(arrived, hidden, residual, copies):
    share = residual.shape[1]
    start = pl.multiple_of(lax.axis_index("dev") * share, 128)
    total = hidden[:, pl.ds(start, share)].astype(f32)
    total = total + jnp.sum(arrived[...].astype(f32), axis=0)
    residual[...] = total
    copies[...] = jnp.broadcast_to(total.astype(bf16)[None], copies.shape)


def add_up(arrived, hidden):
    return pl.pallas_call(
        residual_kernel,
        out_shape=(
            jax.ShapeDtypeStruct(arrived.shape[1:], f32),
            jax.ShapeDtypeStruct(arrived.shape, bf16),
        ),
        in_specs=[VMEM, VMEM],
        out_specs=(VMEM, VMEM),
        compiler_params=pltpu.CompilerParams(vmem_limit_bytes=LIMIT),
        name="residual",
    )(arrived, hidden)


def experts_kernel(
    arrived,
    gain,
    coefficients,
    gate_own,
    gate_other,
    up_own,
    up_other,
    down_own,
    down_other,
    part,
    first,
    second,
    first_arrivals,
    second_arrivals,
):
    pairs, devs, rows, share = arrived.shape
    width = devs * share
    core = lax.axis_index("core")
    copies = []
    for dev in range(devs):
        band = pl.ds(dev * share, share)
        for place, source in enumerate((gate_own, gate_other, up_own, up_other)):
            copy = pltpu.make_async_copy(
                source.at[band], first.at[place, band], first_arrivals.at[place, dev]
            )
            copy.start()
            copies.append(copy)
    down_copies = []
    for place, source in enumerate((down_own, down_other)):
        copy = pltpu.make_async_copy(source, second.at[place], second_arrivals.at[place])
        copy.start()
        down_copies.append(copy)
    squares = jnp.zeros((pairs * rows, 1), f32)
    sums = [jnp.zeros((pairs * rows, first.shape[2]), f32) for _ in range(4)]
    for dev in range(devs):
        value = arrived[:, dev].astype(f32).reshape(pairs * rows, share)
        squares = squares + jnp.sum(value * value, axis=1, keepdims=True)
        value = (value * gain[dev : dev + 1, :]).astype(bf16)
        for place in range(4):
            copies[4 * dev + place].wait()
            sums[place] = sums[place] + jnp.dot(
                value, first[place, dev * share : (dev + 1) * share], preferred_element_type=f32
            )
    factor = lax.rsqrt(squares * (1.0 / width) + 1e-06)
    activated = []
    for place in range(2):
        gate, up = sums[place] * factor, sums[2 + place] * factor
        mix = jnp.where(core == place, coefficients[0], coefficients[1])
        mix = mix.reshape(pairs * rows, NOTES)[:, :1]
        activated.append((gate / (1.0 + jnp.exp(-gate)) * up * mix).astype(bf16))
    for copy in down_copies:
        copy.wait()
    for dev in range(devs):
        columns = slice(dev * share, (dev + 1) * share)
        value = jnp.dot(activated[0], second[0, :, columns], preferred_element_type=f32)
        value = value + jnp.dot(activated[1], second[1, :, columns], preferred_element_type=f32)
        part[:, dev] = value.astype(bf16).reshape(pairs, rows, share)


def experts(arrived, gain, coefficients, *weights):
    pairs, devs, rows, share = arrived.shape
    units = weights[0].shape[1]
    return pl.pallas_call(
        experts_kernel,
        out_shape=jax.ShapeDtypeStruct(arrived.shape, bf16),
        in_specs=[VMEM] * 3 + [ANY] * 6,
        out_specs=VMEM,
        scratch_shapes=[
            pltpu.VMEM((4, devs * share, units), bf16),
            pltpu.VMEM((2, units, devs * share), bf16),
            pltpu.SemaphoreType.DMA((4, devs)),
            pltpu.SemaphoreType.DMA((2,)),
        ],
        compiler_params=pltpu.CompilerParams(vmem_limit_bytes=LIMIT),
        name="experts",
    )(arrived, gain, coefficients, *weights)


def finish_kernel(arrived, residual, out):
    out[...] = residual[...] + jnp.sum(arrived[...].astype(f32), axis=0)


def finish(arrived, residual):
    return pl.pallas_call(
        finish_kernel,
        out_shape=jax.ShapeDtypeStruct(residual.shape, f32),
        in_specs=[VMEM, VMEM],
        out_specs=VMEM,
        compiler_params=pltpu.CompilerParams(vmem_limit_bytes=LIMIT),
        name="finish",
    )(arrived, residual)


def on_device(
    hidden,
    queries,
    latent_cache,
    lengths,
    value_up,
    output_weight,
    norm_gain,
    routes,
    route_scores,
    gate_weight,
    up_weight,
    down_weight,
):
    pairs, devs = lax.axis_size("pair"), lax.axis_size("dev")
    chips = pairs * devs
    rows, model_width = hidden.shape
    share = model_width // devs
    latent = value_up.shape[1]
    weights = [value_up[0], output_weight, gate_weight[0], up_weight[0], down_weight[0]]
    value_up, output_weight, gate_weight, up_weight, down_weight = weights
    value_other, output_other, gate_other, up_other, down_other = [other_core(w) for w in weights]

    parts = attend(
        lengths,
        routes,
        route_scores,
        jnp.swapaxes(queries, 1, 2),
        jnp.swapaxes(latent_cache, 1, 2),
        latent,
    )
    part, coefficients = project(
        exchange(parts), value_up, value_other, output_weight, output_other, pairs, devs
    )
    arrived = exchange(part.reshape(chips, rows, share))
    residual, copies = add_up(arrived, hidden)
    arrived = exchange(copies).reshape(pairs, devs, rows, share)
    part = experts(
        arrived,
        norm_gain.reshape(devs, share),
        coefficients,
        gate_weight,
        gate_other,
        up_weight,
        up_other,
        down_weight,
        down_other,
    )
    return finish(exchange(part.reshape(chips, rows, share)), residual)


def solution(mesh):
    nodes, devs = mesh.devices.shape
    planes = Mesh(mesh.devices.reshape(nodes // 2, 2, devs), ("pair", "core", "dev"))
    node = ("pair", "core")
    both = ("pair", "core", "dev")
    return jax.shard_map(
        on_device,
        mesh=planes,
        in_specs=(
            P(node, None),
            P(node, None, None),
            P(node, "dev", None),
            P(node),
            P(both, None, None),
            P(both, None),
            P(),
            P(node, None),
            P(node, None),
            P(node, None, "dev"),
            P(node, None, "dev"),
            P(node, "dev", None),
        ),
        out_specs=P(node, "dev"),
        check_vma=False,
    )
```

```python
import jax
import jax.numpy as jnp
from jax import lax
from jax.experimental import pallas as pl
from jax.experimental.pallas import tpu as pltpu
from jax.sharding import Mesh
from jax.sharding import PartitionSpec as P

PLANE = ("pair", "dev")
VMEM = pl.BlockSpec(memory_space=pltpu.VMEM)
SMEM = pl.BlockSpec(memory_space=pltpu.SMEM)
ANY = pl.BlockSpec(memory_space=pl.ANY)
NOTES = 128
SLABS = 8
PIECES = 1
LIMIT = 40 * 2**20
f32 = jnp.float32
bf16 = jnp.bfloat16


def exchange(blocks):
    return lax.all_to_all(blocks, PLANE, split_axis=0, concat_axis=0, tiled=True)


def other_core(value):
    return lax.ppermute(value, "core", [(0, 1), (1, 0)])


def thirds(value):
    high = value.astype(bf16).astype(f32)
    rest = value - high
    middle = rest.astype(bf16).astype(f32)
    return high, middle, rest - middle


def attend_kernel(
    lengths_in,
    routes_in,
    scores_in,
    query_in,
    cache,
    out,
    held,
    joined,
    query,
    lengths,
    routes,
    route_scores,
    arrivals,
    small_arrivals,
):
    rows, feature, positions = cache.shape
    heads = query.shape[2]
    tiles = joined.shape[0] - 1
    latent = tiles * NOTES
    dev = lax.axis_index("dev")
    dev_count = lax.axis_size("dev")
    small = [
        pltpu.make_async_copy(source, target, small_arrivals.at[place])
        for place, (source, target) in enumerate(
            (
                (query_in, query),
                (lengths_in, lengths),
                (routes_in, routes),
                (scores_in, route_scores),
            )
        )
    ]
    copies = [
        [
            pltpu.make_async_copy(
                cache.at[row, pl.ds(start, feature // PIECES)],
                held.at[row, pl.ds(start, feature // PIECES)],
                arrivals.at[row],
            )
            for start in range(0, feature, feature // PIECES)
        ]
        for row in range(rows)
    ]
    for copy in small + sum(copies, []):
        copy.start()
    for copy in small:
        copy.wait()
    lane = lax.broadcasted_iota(jnp.int32, (heads, NOTES), 1)
    expert = lax.broadcasted_iota(jnp.int32, (heads, NOTES), 0) // dev_count
    position = lax.broadcasted_iota(jnp.int32, (heads, positions), 1)
    scale = feature**-0.5
    mixes = []
    for row in range(rows):
        total_score = route_scores[row, 0]
        for k in range(1, routes.shape[1]):
            total_score = total_score + route_scores[row, k]
        named = jnp.zeros((heads, NOTES), f32)
        for k in range(routes.shape[1]):
            named = jnp.where(expert == routes[row, k], route_scores[row, k], named)
        mixes.append(2.5 * named / total_score)

    def raw_scores(row):
        pltpu.make_async_copy(cache.at[row], held.at[row], arrivals.at[row]).wait()
        return lax.dot_general(
            query[row], held[row], (((0,), (0,)), ((), ())), preferred_element_type=f32
        )

    following = raw_scores(0)
    for row in range(rows):
        scores = following
        if row + 1 < rows:
            following = raw_scores(row + 1)
        used = lengths[row] - dev * positions
        scores = jnp.where(position < used, scores, -1e30)
        top = jnp.max(scores, axis=1, keepdims=True)
        weights = jnp.exp((scores - top) * scale)
        total = jnp.sum(weights, axis=1, keepdims=True)
        summed = lax.dot_general(
            weights.astype(bf16),
            held[row, :latent, :],
            (((1,), (1,)), ((), ())),
            preferred_element_type=f32,
        )
        mean = summed / total
        log_total = jnp.where(used > 0, top * scale + jnp.log(total), -1e30)
        notes = jnp.zeros((heads, NOTES), f32)
        for place, part in enumerate(thirds(log_total) + thirds(mixes[row])):
            notes = jnp.where(lane == place, part, notes)
        for group in range(heads // 8):
            pair, core = group // 2, group % 2
            target = pl.ds(pair * 64 + core * rows + row, 8, stride=8)
            source = slice(group * 8, group * 8 + 8)
            for tile in range(tiles):
                joined[tile, target] = mean[source, tile * NOTES : (tile + 1) * NOTES]
            joined[tiles, target] = notes[source]
    for tile in range(tiles + 1):
        columns = slice(tile * NOTES, (tile + 1) * NOTES)
        out[:, :, columns] = joined[tile].astype(bf16).reshape(out.shape[0], out.shape[1], NOTES)


def pinned(value, space=pltpu.HBM):
    return pltpu.with_memory_space_constraint(value, space)


def attend(lengths, routes, route_scores, queries, cache, latent):
    rows, feature, positions = cache.shape
    heads = queries.shape[2]
    return pl.pallas_call(
        attend_kernel,
        out_shape=jax.ShapeDtypeStruct((heads // 2, 2 * rows, latent + NOTES), bf16),
        in_specs=[ANY] * 5,
        out_specs=VMEM,
        scratch_shapes=[
            pltpu.VMEM((rows, feature, positions), bf16),
            pltpu.VMEM((latent // NOTES + 1, heads * rows, NOTES), f32),
            pltpu.VMEM(queries.shape, bf16),
            pltpu.SMEM(lengths.shape, jnp.int32),
            pltpu.SMEM(routes.shape, jnp.int32),
            pltpu.SMEM(route_scores.shape, f32),
            pltpu.SemaphoreType.DMA((rows,)),
            pltpu.SemaphoreType.DMA((4,)),
        ],
        compiler_params=pltpu.CompilerParams(vmem_limit_bytes=LIMIT),
        cost_estimate=pl.CostEstimate(
            flops=4 * rows * heads * feature * positions,
            bytes_accessed=2 * rows * feature * positions,
            transcendentals=rows * heads * positions,
        ),
        name="attend",
    )(*[pinned(value) for value in (lengths, routes, route_scores, queries, cache)])


def project_kernel(
    arrived, up_own, up_other, out_own, other_in, part, coefficients, out_other, arrivals
):
    copies = []
    for cut in range(SLABS):
        band = pl.ds(cut * (out_other.shape[0] // SLABS), out_other.shape[0] // SLABS)
        copies.append(
            pltpu.make_async_copy(other_in.at[band], out_other.at[band], arrivals.at[cut])
        )
        copies[-1].start()
    pairs, devs, rows, share = part.shape
    latent = up_own.shape[0]
    core = lax.axis_index("core")
    notes = arrived[:, :, latent:].astype(f32)
    lane = lax.broadcasted_iota(jnp.int32, notes.shape, 2)
    log_total = jnp.sum(jnp.where(lane < 3, notes, 0.0), axis=2, keepdims=True)
    coefficient = jnp.sum(
        jnp.where((lane >= 3) & (lane < 6), notes, 0.0), axis=2, keepdims=True
    )
    coefficient = coefficient.reshape(pairs, devs, 2 * rows, 1)[:, 0]
    coefficient = jnp.broadcast_to(coefficient, (pairs, 2 * rows, NOTES))
    coefficients[0] = coefficient[:, :rows]
    coefficients[1] = coefficient[:, rows:]
    log_total = log_total.reshape(pairs, devs, 2 * rows, 1)
    weight = jnp.exp(log_total - jnp.max(log_total, axis=1, keepdims=True))
    weight = weight / jnp.sum(weight, axis=1, keepdims=True)
    values = arrived[:, :, :latent].reshape(pairs, devs, 2 * rows, latent)
    attended = weight[:, 0] * values[:, 0].astype(f32)
    for dev in range(1, devs):
        attended = attended + weight[:, dev] * values[:, dev].astype(f32)
    attended = attended.reshape(pairs * 2 * rows, latent).astype(bf16)

    def head(up, is_own):
        value = jnp.dot(attended, up[...], preferred_element_type=f32)
        value = value.reshape(pairs, 2 * rows, -1)
        low, high = value[:, :rows], value[:, rows:]
        picked = jnp.where(core == (0 if is_own else 1), low, high)
        return picked.reshape(pairs * rows, -1).astype(bf16)

    own, other = head(up_own, True), head(up_other, False)
    for copy in copies:
        copy.wait()
    for dev in range(devs):
        columns = slice(dev * share, (dev + 1) * share)
        value = jnp.dot(own, out_own[:, columns], preferred_element_type=f32)
        value = value + jnp.dot(other, out_other[:, columns], preferred_element_type=f32)
        part[:, dev] = value.astype(bf16).reshape(pairs, rows, share)


def project(arrived, up_own, up_other, out_own, out_other, pairs, devs):
    rows = arrived.shape[1] // 2
    width = out_own.shape[1]
    return pl.pallas_call(
        project_kernel,
        out_shape=(
            jax.ShapeDtypeStruct((pairs, devs, rows, width // devs), bf16),
            jax.ShapeDtypeStruct((2, pairs, rows, NOTES), f32),
        ),
        in_specs=[VMEM] * 4 + [ANY],
        out_specs=(VMEM, VMEM),
        scratch_shapes=[
            pltpu.VMEM(out_other.shape, bf16),
            pltpu.SemaphoreType.DMA((SLABS,)),
        ],
        compiler_params=pltpu.CompilerParams(vmem_limit_bytes=LIMIT),
        name="project",
    )(arrived, up_own, up_other, out_own, pinned(out_other))


def residual_kernel(arrived, hidden, residual, copies):
    share = residual.shape[1]
    start = pl.multiple_of(lax.axis_index("dev") * share, 128)
    total = hidden[:, pl.ds(start, share)].astype(f32)
    total = total + jnp.sum(arrived[...].astype(f32), axis=0)
    residual[...] = total
    copies[...] = jnp.broadcast_to(total.astype(bf16)[None], copies.shape)


def add_up(arrived, hidden):
    return pl.pallas_call(
        residual_kernel,
        out_shape=(
            jax.ShapeDtypeStruct(arrived.shape[1:], f32),
            jax.ShapeDtypeStruct(arrived.shape, bf16),
        ),
        in_specs=[VMEM, VMEM],
        out_specs=(VMEM, VMEM),
        compiler_params=pltpu.CompilerParams(vmem_limit_bytes=LIMIT),
        name="residual",
    )(arrived, hidden)


def experts_kernel(
    arrived,
    gain,
    coefficients,
    gate_own,
    gate_other,
    up_own,
    up_other,
    down_own,
    down_other,
    part,
    first,
    second,
    first_arrivals,
    second_arrivals,
):
    pairs, devs, rows, share = arrived.shape
    width = devs * share
    units = first.shape[2]
    core = lax.axis_index("core")
    first_copies, second_copies = [], []
    for dev in range(devs):
        band = pl.ds(dev * share, share)
        for place, source in enumerate((gate_own, gate_other, up_own, up_other)):
            first_copies.append(
                pltpu.make_async_copy(
                    source.at[band], first.at[place, band], first_arrivals.at[place, dev]
                )
            )
    for place, source in enumerate((down_own, down_other)):
        for cut in range(SLABS):
            band = pl.ds(cut * (units // SLABS), units // SLABS)
            second_copies.append(
                pltpu.make_async_copy(
                    source.at[band], second.at[place, band], second_arrivals.at[place, cut]
                )
            )
    for copy in first_copies + second_copies:
        copy.start()
    squares = jnp.zeros((pairs * rows, 1), f32)
    sums = [jnp.zeros((pairs * rows, units), f32) for _ in range(4)]
    for dev in range(devs):
        value = arrived[:, dev].astype(f32).reshape(pairs * rows, share)
        squares = squares + jnp.sum(value * value, axis=1, keepdims=True)
        value = (value * gain[dev : dev + 1, :]).astype(bf16)
        for place in range(4):
            first_copies[4 * dev + place].wait()
        for place in range(4):
            sums[place] = sums[place] + jnp.dot(
                value, first[place, dev * share : (dev + 1) * share], preferred_element_type=f32
            )
    factor = lax.rsqrt(squares * (1.0 / width) + 1e-06)
    activated = []
    for place in range(2):
        gate, up = sums[place] * factor, sums[2 + place] * factor
        mix = jnp.where(core == place, coefficients[0], coefficients[1])
        mix = mix.reshape(pairs * rows, NOTES)[:, :1]
        activated.append((gate / (1.0 + jnp.exp(-gate)) * up * mix).astype(bf16))
    for copy in second_copies:
        copy.wait()
    for dev in range(devs):
        columns = slice(dev * share, (dev + 1) * share)
        value = jnp.dot(activated[0], second[0, :, columns], preferred_element_type=f32)
        value = value + jnp.dot(activated[1], second[1, :, columns], preferred_element_type=f32)
        part[:, dev] = value.astype(bf16).reshape(pairs, rows, share)


def experts(arrived, gain, coefficients, *weights):
    pairs, devs, rows, share = arrived.shape
    units = weights[0].shape[1]
    return pl.pallas_call(
        experts_kernel,
        out_shape=jax.ShapeDtypeStruct(arrived.shape, bf16),
        in_specs=[VMEM] * 3 + [ANY] * 6,
        out_specs=VMEM,
        scratch_shapes=[
            pltpu.VMEM((4, devs * share, units), bf16),
            pltpu.VMEM((2, units, devs * share), bf16),
            pltpu.SemaphoreType.DMA((4, devs)),
            pltpu.SemaphoreType.DMA((2, SLABS)),
        ],
        compiler_params=pltpu.CompilerParams(vmem_limit_bytes=LIMIT),
        name="experts",
    )(arrived, gain, coefficients, *[pinned(weight) for weight in weights])


def finish_kernel(arrived, residual, out):
    out[...] = residual[...] + jnp.sum(arrived[...].astype(f32), axis=0)


def finish(arrived, residual):
    return pl.pallas_call(
        finish_kernel,
        out_shape=jax.ShapeDtypeStruct(residual.shape, f32),
        in_specs=[VMEM, VMEM],
        out_specs=VMEM,
        compiler_params=pltpu.CompilerParams(vmem_limit_bytes=LIMIT),
        name="finish",
    )(arrived, residual)


def on_device(
    hidden,
    queries,
    latent_cache,
    lengths,
    value_up,
    output_weight,
    norm_gain,
    routes,
    route_scores,
    gate_weight,
    up_weight,
    down_weight,
):
    pairs, devs = lax.axis_size("pair"), lax.axis_size("dev")
    chips = pairs * devs
    rows, model_width = hidden.shape
    share = model_width // devs
    latent = value_up.shape[1]
    value_up, gate_weight, up_weight, down_weight = (
        value_up[0],
        gate_weight[0],
        up_weight[0],
        down_weight[0],
    )
    value_other, output_other, gate_other, up_other, down_other = [
        other_core(weight)
        for weight in (value_up, output_weight, gate_weight, up_weight, down_weight)
    ]
    parts = attend(
        lengths,
        routes,
        route_scores,
        jnp.swapaxes(queries, 1, 2),
        jnp.swapaxes(latent_cache, 1, 2),
        latent,
    )
    part, coefficients = project(
        exchange(parts), value_up, value_other, output_weight, output_other, pairs, devs
    )
    arrived = exchange(part.reshape(chips, rows, share))
    residual, copies = add_up(arrived, hidden)
    arrived = exchange(copies).reshape(pairs, devs, rows, share)
    part = experts(
        arrived,
        norm_gain.reshape(devs, share),
        coefficients,
        gate_weight,
        gate_other,
        up_weight,
        up_other,
        down_weight,
        down_other,
    )
    return finish(exchange(part.reshape(chips, rows, share)), residual)


def solution(mesh):
    nodes, devs = mesh.devices.shape
    planes = Mesh(mesh.devices.reshape(nodes // 2, 2, devs), ("pair", "core", "dev"))
    node = ("pair", "core")
    both = ("pair", "core", "dev")
    return jax.shard_map(
        on_device,
        mesh=planes,
        in_specs=(
            P(node, None),
            P(node, None, None),
            P(node, "dev", None),
            P(node),
            P(both, None, None),
            P(both, None),
            P(),
            P(node, None),
            P(node, None),
            P(node, None, "dev"),
            P(node, None, "dev"),
            P(node, "dev", None),
        ),
        out_specs=P(node, "dev"),
        check_vma=False,
    )
```

```python
import jax
import jax.numpy as jnp
from jax import lax
from jax.experimental import pallas as pl
from jax.experimental.pallas import tpu as pltpu
from jax.sharding import Mesh
from jax.sharding import PartitionSpec as P

PLANE = ("pair", "dev")
VMEM = pl.BlockSpec(memory_space=pltpu.VMEM)
SMEM = pl.BlockSpec(memory_space=pltpu.SMEM)
ANY = pl.BlockSpec(memory_space=pl.ANY)
NOTES = 128
SLABS = 2
STAGED = 6
EARLY = 4
CHUNK = 256
LOOK = False
WINDOW = 16
LOG2E = 1.4426950408889634
LIMIT = 40 * 2**20
f32 = jnp.float32
bf16 = jnp.bfloat16


def exchange(blocks):
    return lax.all_to_all(blocks, PLANE, split_axis=0, concat_axis=0, tiled=True)


def other_core(value):
    return lax.ppermute(value, "core", [(0, 1), (1, 0)])


def thirds(value):
    high = value.astype(bf16).astype(f32)
    rest = value - high
    middle = rest.astype(bf16).astype(f32)
    return high, middle, rest - middle


def attend_kernel(
    lengths_in,
    routes_in,
    scores_in,
    query_in,
    cache,
    out,
    held,
    joined,
    query,
    lengths,
    routes,
    route_scores,
    arrivals,
    small_arrivals,
    query_arrivals,
):
    rows, feature, positions = cache.shape
    heads = query.shape[2]
    tiles = joined.shape[0] - 1
    latent = tiles * NOTES
    dev = lax.axis_index("dev")
    dev_count = lax.axis_size("dev")
    small = [
        pltpu.make_async_copy(source, target, small_arrivals.at[place])
        for place, (source, target) in enumerate(
            (
                (lengths_in, lengths),
                (routes_in, routes),
                (scores_in, route_scores),
            )
        )
    ]
    query_copies = [
        pltpu.make_async_copy(query_in.at[row], query.at[row], query_arrivals.at[row])
        for row in range(rows)
    ]
    copies = [
        pltpu.make_async_copy(cache.at[row], held.at[row], arrivals.at[row]) for row in range(rows)
    ]
    query_copies[0].start()
    copies[0].start()
    for copy in small + query_copies[1:] + copies[1:EARLY]:
        copy.start()
    lane = lax.broadcasted_iota(jnp.int32, (heads, NOTES), 1)
    expert = lax.broadcasted_iota(jnp.int32, (heads, NOTES), 0) // dev_count
    position = lax.broadcasted_iota(jnp.int32, (1, positions), 1)
    scale = feature**-0.5
    for copy in small:
        copy.wait()
    mixes = []
    for row in range(rows):
        total_score = route_scores[row, 0]
        for k in range(1, routes.shape[1]):
            total_score = total_score + route_scores[row, k]
        named = jnp.zeros((heads, NOTES), f32)
        for k in range(routes.shape[1]):
            named = jnp.where(expert == routes[row, k], route_scores[row, k], named)
        mixes.append(2.5 * named / total_score)

    def raw_scores(row):
        query_copies[row].wait()
        copies[row].wait()
        for copy in copies[row + EARLY : row + EARLY + 1]:
            copy.start()
        return lax.dot_general(
            query[row], held[row], (((0,), (0,)), ((), ())), preferred_element_type=f32
        )

    following = raw_scores(0)
    for row in range(rows):
        scores = following
        if LOOK and row + 1 < rows:
            following = raw_scores(row + 1)
        used = lengths[row] - dev * positions
        scores = scores + jnp.where(position < used, 0.0, -1e30)
        top = jnp.max(scores, axis=1, keepdims=True)
        total, summed = 0.0, 0.0
        for start in range(0, positions, CHUNK):
            weights = jnp.exp2((scores[:, start : start + CHUNK] - top) * (scale * LOG2E))
            total = total + jnp.sum(weights, axis=1, keepdims=True)
            summed = summed + lax.dot_general(
                weights.astype(bf16),
                held[row, :latent, start : start + CHUNK],
                (((1,), (1,)), ((), ())),
                preferred_element_type=f32,
            )
        mean = summed / total
        log_total = jnp.where(used > 0, top * scale + jnp.log(total), -1e30)
        notes = jnp.zeros((heads, NOTES), f32)
        for place, part in enumerate(thirds(log_total) + thirds(mixes[row])):
            notes = jnp.where(lane == place, part, notes)
        for group in range(heads // 8):
            pair, core = group // 2, group % 2
            target = pl.ds(pair * 64 + core * rows + row, 8, stride=8)
            source = slice(group * 8, group * 8 + 8)
            for tile in range(tiles):
                joined[tile, target] = mean[source, tile * NOTES : (tile + 1) * NOTES]
            joined[tiles, target] = notes[source]
        if not LOOK and row + 1 < rows:
            following = raw_scores(row + 1)
    for tile in range(tiles + 1):
        columns = slice(tile * NOTES, (tile + 1) * NOTES)
        out[:, :, columns] = joined[tile].astype(bf16).reshape(out.shape[0], out.shape[1], NOTES)


def pinned(value, space=pltpu.HBM):
    return pltpu.with_memory_space_constraint(value, space)


def attend(lengths, routes, route_scores, queries, cache, latent):
    rows, feature, positions = cache.shape
    heads = queries.shape[2]
    return pl.pallas_call(
        attend_kernel,
        out_shape=pltpu.VMEM((heads // 2, 2 * rows, latent + NOTES), bf16),
        in_specs=[ANY] * 5,
        out_specs=VMEM,
        scratch_shapes=[
            pltpu.VMEM((rows, feature, positions), bf16),
            pltpu.VMEM((latent // NOTES + 1, heads * rows, NOTES), f32),
            pltpu.VMEM(queries.shape, bf16),
            pltpu.SMEM(lengths.shape, jnp.int32),
            pltpu.SMEM(routes.shape, jnp.int32),
            pltpu.SMEM(route_scores.shape, f32),
            pltpu.SemaphoreType.DMA((rows,)),
            pltpu.SemaphoreType.DMA((3,)),
            pltpu.SemaphoreType.DMA((rows,)),
        ],
        compiler_params=pltpu.CompilerParams(vmem_limit_bytes=LIMIT),
        cost_estimate=pl.CostEstimate(
            flops=4 * rows * heads * feature * positions,
            bytes_accessed=2 * rows * feature * positions,
            transcendentals=rows * heads * positions,
        ),
        name="attend",
    )(*[pinned(value) for value in (lengths, routes, route_scores, queries, cache)])


def project_kernel(
    arrived, up_own, up_other, out_own, other_in, part, coefficients, out_other, arrivals
):
    copies = []
    for cut in range(SLABS):
        band = pl.ds(cut * (out_other.shape[0] // SLABS), out_other.shape[0] // SLABS)
        copies.append(
            pltpu.make_async_copy(other_in.at[band], out_other.at[band], arrivals.at[cut])
        )
        copies[-1].start()
    pairs, devs, rows, share = part.shape
    latent = up_own.shape[0]
    core = lax.axis_index("core")
    notes = arrived[:, :, latent:].astype(f32)
    lane = lax.broadcasted_iota(jnp.int32, notes.shape, 2)
    log_total = jnp.sum(jnp.where(lane < 3, notes, 0.0), axis=2, keepdims=True)
    coefficient = jnp.sum(
        jnp.where((lane >= 3) & (lane < 6), notes, 0.0), axis=2, keepdims=True
    )
    coefficient = coefficient.reshape(pairs, devs, 2 * rows, 1)[:, 0]
    coefficient = jnp.broadcast_to(coefficient, (pairs, 2 * rows, NOTES))
    coefficients[0] = coefficient[:, :rows]
    coefficients[1] = coefficient[:, rows:]
    log_total = log_total.reshape(pairs, devs, 2 * rows, 1)
    weight = jnp.exp(log_total - jnp.max(log_total, axis=1, keepdims=True))
    weight = weight / jnp.sum(weight, axis=1, keepdims=True)
    values = arrived[:, :, :latent].reshape(pairs, devs, 2 * rows, latent)
    attended = weight[:, 0] * values[:, 0].astype(f32)
    for dev in range(1, devs):
        attended = attended + weight[:, dev] * values[:, dev].astype(f32)
    attended = attended.reshape(pairs * 2 * rows, latent).astype(bf16)

    def head(up, is_own):
        value = jnp.dot(attended, up[...], preferred_element_type=f32)
        value = value.reshape(pairs, 2 * rows, -1)
        low, high = value[:, :rows], value[:, rows:]
        picked = jnp.where(core == (0 if is_own else 1), low, high)
        return picked.reshape(pairs * rows, -1).astype(bf16)

    own, other = head(up_own, True), head(up_other, False)
    for copy in copies:
        copy.wait()
    for dev in range(devs):
        columns = slice(dev * share, (dev + 1) * share)
        value = jnp.dot(own, out_own[:, columns], preferred_element_type=f32)
        value = value + jnp.dot(other, out_other[:, columns], preferred_element_type=f32)
        part[:, dev] = value.astype(bf16).reshape(pairs, rows, share)


def project(arrived, up_own, up_other, out_own, out_other, pairs, devs):
    rows = arrived.shape[1] // 2
    width = out_own.shape[1]
    return pl.pallas_call(
        project_kernel,
        out_shape=(
            jax.ShapeDtypeStruct((pairs, devs, rows, width // devs), bf16),
            jax.ShapeDtypeStruct((2, pairs, rows, NOTES), f32),
        ),
        in_specs=[VMEM] * 4 + [ANY],
        out_specs=(VMEM, VMEM),
        scratch_shapes=[
            pltpu.VMEM(out_other.shape, bf16),
            pltpu.SemaphoreType.DMA((SLABS,)),
        ],
        compiler_params=pltpu.CompilerParams(vmem_limit_bytes=LIMIT),
        name="project",
    )(arrived, up_own, up_other, out_own, pinned(out_other))


def residual_kernel(arrived, hidden, residual, copies):
    share = residual.shape[1]
    start = pl.multiple_of(lax.axis_index("dev") * share, 128)
    total = hidden[:, pl.ds(start, share)].astype(f32)
    total = total + jnp.sum(arrived[...].astype(f32), axis=0)
    residual[...] = total
    copies[...] = jnp.broadcast_to(total.astype(bf16)[None], copies.shape)


def add_up(arrived, hidden):
    return pl.pallas_call(
        residual_kernel,
        out_shape=(
            jax.ShapeDtypeStruct(arrived.shape[1:], f32),
            pltpu.VMEM(arrived.shape, bf16),
        ),
        in_specs=[VMEM, VMEM],
        out_specs=(VMEM, VMEM),
        compiler_params=pltpu.CompilerParams(vmem_limit_bytes=LIMIT),
        name="residual",
    )(arrived, hidden)


def stage_kernel(after, gate_own, gate_other, up_own, up_other, out, arrivals):
    share = out.shape[1]
    copies = []
    for place in range(out.shape[0]):
        source = (gate_own, gate_other, up_own, up_other)[place % 4]
        copies.append(
            pltpu.make_async_copy(
                source.at[pl.ds(place // 4 * share, share)], out.at[place], arrivals.at[place]
            )
        )
    for copy in copies:
        copy.start()
    for copy in copies:
        copy.wait()


def stage(after, share, *weights):
    return pl.pallas_call(
        stage_kernel,
        out_shape=pltpu.VMEM((STAGED, share, weights[0].shape[1]), bf16),
        in_specs=[ANY] * 5,
        out_specs=VMEM,
        scratch_shapes=[pltpu.SemaphoreType.DMA((STAGED,))],
        compiler_params=pltpu.CompilerParams(vmem_limit_bytes=4 * 2**20),
        cost_estimate=pl.CostEstimate(
            flops=0, bytes_accessed=4 * STAGED * share * weights[0].shape[1], transcendentals=0
        ),
        name="stage",
    )(after, *[pinned(weight) for weight in weights])


def experts_kernel(
    arrived,
    gain,
    coefficients,
    staged,
    gate_own,
    gate_other,
    up_own,
    up_other,
    down_own,
    down_other,
    part,
    first,
    second,
    first_arrivals,
    second_arrivals,
):
    pairs, devs, rows, share = arrived.shape
    width = devs * share
    units = first.shape[2]
    core = lax.axis_index("core")
    copies = []
    for dev in range(devs):
        band = pl.ds(dev * share, share)
        for place, source in enumerate((gate_own, gate_other, up_own, up_other)):
            copies.append(
                pltpu.make_async_copy(
                    source.at[band], first.at[place, band], first_arrivals.at[place, dev]
                )
            )
    for dev in range(devs):
        band = pl.ds(dev * share, share)
        for place, source in enumerate((down_own, down_other)):
            copies.append(
                pltpu.make_async_copy(
                    source.at[:, band], second.at[place, :, band], second_arrivals.at[place, dev]
                )
            )
    copies = copies[STAGED:]
    begun = [copy.start() for copy in copies[:WINDOW]]
    arrived_count = 0

    def receive(until):
        nonlocal arrived_count
        while arrived_count < until - STAGED:
            copies[arrived_count].wait()
            arrived_count += 1
            if len(begun) < len(copies):
                begun.append(copies[len(begun)].start())

    squares = jnp.zeros((pairs * rows, 1), f32)
    sums = [jnp.zeros((pairs * rows, units), f32) for _ in range(4)]
    for dev in range(devs):
        value = arrived[:, dev].astype(f32).reshape(pairs * rows, share)
        squares = squares + jnp.sum(value * value, axis=1, keepdims=True)
        value = (value * gain[dev : dev + 1, :]).astype(bf16)
        receive(4 * dev + 4)
        for place in range(4):
            if 4 * dev + place < STAGED:
                band = staged[4 * dev + place]
            else:
                band = first[place, dev * share : (dev + 1) * share]
            sums[place] = sums[place] + jnp.dot(value, band, preferred_element_type=f32)
    factor = lax.rsqrt(squares * (1.0 / width) + 1e-06)
    activated = []
    for place in range(2):
        gate, up = sums[place] * factor, sums[2 + place] * factor
        mix = jnp.where(core == place, coefficients[0], coefficients[1])
        mix = mix.reshape(pairs * rows, NOTES)[:, :1]
        activated.append((gate / (1.0 + jnp.exp(-gate)) * up * mix).astype(bf16))
    for dev in range(devs):
        receive(4 * devs + 2 * dev + 2)
        columns = slice(dev * share, (dev + 1) * share)
        value = jnp.dot(activated[0], second[0, :, columns], preferred_element_type=f32)
        value = value + jnp.dot(activated[1], second[1, :, columns], preferred_element_type=f32)
        part[:, dev] = value.astype(bf16).reshape(pairs, rows, share)


def experts(arrived, gain, coefficients, staged, *weights):
    pairs, devs, rows, share = arrived.shape
    units = weights[0].shape[1]
    return pl.pallas_call(
        experts_kernel,
        out_shape=jax.ShapeDtypeStruct(arrived.shape, bf16),
        in_specs=[VMEM] * 4 + [ANY] * 6,
        out_specs=VMEM,
        scratch_shapes=[
            pltpu.VMEM((4, devs * share, units), bf16),
            pltpu.VMEM((2, units, devs * share), bf16),
            pltpu.SemaphoreType.DMA((4, devs)),
            pltpu.SemaphoreType.DMA((2, devs)),
        ],
        compiler_params=pltpu.CompilerParams(vmem_limit_bytes=LIMIT),
        name="experts",
    )(
        arrived,
        gain,
        coefficients,
        pinned(staged, pltpu.VMEM),
        *[pinned(weight) for weight in weights],
    )


def finish_kernel(arrived, residual, out):
    out[...] = residual[...] + jnp.sum(arrived[...].astype(f32), axis=0)


def finish(arrived, residual):
    return pl.pallas_call(
        finish_kernel,
        out_shape=jax.ShapeDtypeStruct(residual.shape, f32),
        in_specs=[VMEM, VMEM],
        out_specs=VMEM,
        compiler_params=pltpu.CompilerParams(vmem_limit_bytes=LIMIT),
        name="finish",
    )(arrived, residual)


def on_device(
    hidden,
    queries,
    latent_cache,
    lengths,
    value_up,
    output_weight,
    norm_gain,
    routes,
    route_scores,
    gate_weight,
    up_weight,
    down_weight,
):
    pairs, devs = lax.axis_size("pair"), lax.axis_size("dev")
    chips = pairs * devs
    rows, model_width = hidden.shape
    share = model_width // devs
    latent = value_up.shape[1]
    value_up, gate_weight, up_weight, down_weight = (
        value_up[0],
        gate_weight[0],
        up_weight[0],
        down_weight[0],
    )
    value_other, output_other, gate_other, up_other, down_other = [
        other_core(weight)
        for weight in (value_up, output_weight, gate_weight, up_weight, down_weight)
    ]
    parts = attend(
        lengths,
        routes,
        route_scores,
        jnp.swapaxes(queries, 1, 2),
        jnp.swapaxes(latent_cache, 1, 2),
        latent,
    )
    part, coefficients = project(
        exchange(parts), value_up, value_other, output_weight, output_other, pairs, devs
    )
    arrived = exchange(part.reshape(chips, rows, share))
    residual, copies = add_up(arrived, hidden)
    staged = stage(residual, share, gate_weight, gate_other, up_weight, up_other)
    arrived = exchange(copies).reshape(pairs, devs, rows, share)
    part = experts(
        arrived,
        norm_gain.reshape(devs, share),
        coefficients,
        staged,
        gate_weight,
        gate_other,
        up_weight,
        up_other,
        down_weight,
        down_other,
    )
    return finish(exchange(part.reshape(chips, rows, share)), residual)


def solution(mesh):
    nodes, devs = mesh.devices.shape
    planes = Mesh(mesh.devices.reshape(nodes // 2, 2, devs), ("pair", "core", "dev"))
    node = ("pair", "core")
    both = ("pair", "core", "dev")
    return jax.shard_map(
        on_device,
        mesh=planes,
        in_specs=(
            P(node, None),
            P(node, None, None),
            P(node, "dev", None),
            P(node),
            P(both, None, None),
            P(both, None),
            P(),
            P(node, None),
            P(node, None),
            P(node, None, "dev"),
            P(node, None, "dev"),
            P(node, "dev", None),
        ),
        out_specs=P(node, "dev"),
        check_vma=False,
    )
```

```python
import functools

import jax
import jax.numpy as jnp
from jax import lax
from jax.experimental import pallas as pl
from jax.experimental.pallas import tpu as pltpu
from jax.sharding import Mesh
from jax.sharding import PartitionSpec as P

PLANE = ("pair", "dev")
VMEM = pl.BlockSpec(memory_space=pltpu.VMEM)
SMEM = pl.BlockSpec(memory_space=pltpu.SMEM)
ANY = pl.BlockSpec(memory_space=pl.ANY)
NOTES = 128
SLABS = 2
STAGED = 6
EARLY = 4
CHUNK = 256
LOOK = False
WINDOW = 16
LOG2E = 1.4426950408889634
LIMIT = 40 * 2**20
f32 = jnp.float32
bf16 = jnp.bfloat16


def exchange(blocks):
    return lax.all_to_all(blocks, PLANE, split_axis=0, concat_axis=0, tiled=True)


def other_core(value):
    return lax.ppermute(value, "core", [(0, 1), (1, 0)])


def thirds(value):
    high = value.astype(bf16).astype(f32)
    rest = value - high
    middle = rest.astype(bf16).astype(f32)
    return high, middle, rest - middle


def attend_kernel(
    lengths_in,
    routes_in,
    scores_in,
    query_in,
    cache,
    out,
    held,
    joined,
    query,
    lengths,
    routes,
    route_scores,
    arrivals,
    small_arrivals,
    query_arrivals,
):
    rows, feature, positions = cache.shape
    heads = query.shape[2]
    tiles = joined.shape[0] - 1
    latent = tiles * NOTES
    dev = lax.axis_index("dev")
    dev_count = lax.axis_size("dev")
    small = [
        pltpu.make_async_copy(source, target, small_arrivals.at[place])
        for place, (source, target) in enumerate(
            (
                (lengths_in, lengths),
                (routes_in, routes),
                (scores_in, route_scores),
            )
        )
    ]
    query_copies = [
        pltpu.make_async_copy(query_in.at[row], query.at[row], query_arrivals.at[row])
        for row in range(rows)
    ]
    copies = [
        pltpu.make_async_copy(cache.at[row], held.at[row], arrivals.at[row]) for row in range(rows)
    ]
    for copy in query_copies[:1] + copies[:1] + small + query_copies[1:] + copies[1:]:
        copy.start()
    lane = lax.broadcasted_iota(jnp.int32, (heads, NOTES), 1)
    expert = lax.broadcasted_iota(jnp.int32, (heads, NOTES), 0) // dev_count
    position = lax.broadcasted_iota(jnp.int32, (1, positions), 1)
    scale = feature**-0.5
    for copy in small:
        copy.wait()

    def one_row(row, carry):
        total_score = route_scores[row, 0]
        for k in range(1, routes.shape[1]):
            total_score = total_score + route_scores[row, k]
        named = jnp.zeros((heads, NOTES), f32)
        for k in range(routes.shape[1]):
            named = jnp.where(expert == routes[row, k], route_scores[row, k], named)
        mix = 2.5 * named / total_score
        used = lengths[row] - dev * positions
        pltpu.make_async_copy(query_in.at[row], query.at[row], query_arrivals.at[row]).wait()
        pltpu.make_async_copy(cache.at[row], held.at[row], arrivals.at[row]).wait()

        def store(mean, log_total):
            notes = jnp.zeros((heads, NOTES), f32)
            for place, part in enumerate(thirds(log_total) + thirds(mix)):
                notes = jnp.where(lane == place, part, notes)
            for group in range(heads // 8):
                pair, core = group // 2, group % 2
                target = pl.ds(pair * 64 + core * rows + row, 8, stride=8)
                source = slice(group * 8, group * 8 + 8)
                for tile in range(tiles):
                    joined[tile, target] = mean[source, tile * NOTES : (tile + 1) * NOTES]
                joined[tiles, target] = notes[source]

        @pl.when(used > 0)
        def _():
            scores = lax.dot_general(
                query[row], held[row], (((0,), (0,)), ((), ())), preferred_element_type=f32
            )
            scores = scores + jnp.where(position < used, 0.0, -1e30)
            top = jnp.max(scores, axis=1, keepdims=True)
            total, summed = 0.0, 0.0
            for start in range(0, positions, CHUNK):
                weights = jnp.exp2((scores[:, start : start + CHUNK] - top) * (scale * LOG2E))
                total = total + jnp.sum(weights, axis=1, keepdims=True)
                summed = summed + lax.dot_general(
                    weights.astype(bf16),
                    held[row, :latent, start : start + CHUNK],
                    (((1,), (1,)), ((), ())),
                    preferred_element_type=f32,
                )
            store(summed / total, top * scale + jnp.log(total))

        @pl.when(used <= 0)
        def _():
            store(jnp.zeros((heads, latent), f32), jnp.full((heads, 1), -1e30, f32))

        return carry

    lax.fori_loop(0, rows, one_row, 0)
    for tile in range(tiles + 1):
        columns = slice(tile * NOTES, (tile + 1) * NOTES)
        out[:, :, columns] = joined[tile].astype(bf16).reshape(out.shape[0], out.shape[1], NOTES)


def pinned(value, space=pltpu.HBM):
    return pltpu.with_memory_space_constraint(value, space)


def attend(lengths, routes, route_scores, queries, cache, latent):
    rows, feature, positions = cache.shape
    heads = queries.shape[2]
    return pl.pallas_call(
        attend_kernel,
        out_shape=pltpu.VMEM((heads // 2, 2 * rows, latent + NOTES), bf16),
        in_specs=[ANY] * 5,
        out_specs=VMEM,
        scratch_shapes=[
            pltpu.VMEM((rows, feature, positions), bf16),
            pltpu.VMEM((latent // NOTES + 1, heads * rows, NOTES), f32),
            pltpu.VMEM(queries.shape, bf16),
            pltpu.SMEM(lengths.shape, jnp.int32),
            pltpu.SMEM(routes.shape, jnp.int32),
            pltpu.SMEM(route_scores.shape, f32),
            pltpu.SemaphoreType.DMA((rows,)),
            pltpu.SemaphoreType.DMA((3,)),
            pltpu.SemaphoreType.DMA((rows,)),
        ],
        compiler_params=pltpu.CompilerParams(vmem_limit_bytes=LIMIT),
        cost_estimate=pl.CostEstimate(
            flops=4 * rows * heads * feature * positions,
            bytes_accessed=2 * rows * feature * positions,
            transcendentals=rows * heads * positions,
        ),
        name="attend",
    )(*[pinned(value) for value in (lengths, routes, route_scores, queries, cache)])


def project_kernel(
    arrived, up_own, up_other, out_own, other_in, part, coefficients, out_other, arrivals
):
    copies = []
    for cut in range(SLABS):
        band = pl.ds(cut * (out_other.shape[0] // SLABS), out_other.shape[0] // SLABS)
        copies.append(
            pltpu.make_async_copy(other_in.at[band], out_other.at[band], arrivals.at[cut])
        )
        copies[-1].start()
    pairs, devs, rows, share = part.shape
    latent = up_own.shape[0]
    core = lax.axis_index("core")
    notes = arrived[:, :, latent:].astype(f32)
    lane = lax.broadcasted_iota(jnp.int32, notes.shape, 2)
    log_total = jnp.sum(jnp.where(lane < 3, notes, 0.0), axis=2, keepdims=True)
    coefficient = jnp.sum(
        jnp.where((lane >= 3) & (lane < 6), notes, 0.0), axis=2, keepdims=True
    )
    coefficient = coefficient.reshape(pairs, devs, 2 * rows, 1)[:, 0]
    coefficient = jnp.broadcast_to(coefficient, (pairs, 2 * rows, NOTES))
    coefficients[0] = coefficient[:, :rows]
    coefficients[1] = coefficient[:, rows:]
    log_total = log_total.reshape(pairs, devs, 2 * rows, 1)
    weight = jnp.exp(log_total - jnp.max(log_total, axis=1, keepdims=True))
    weight = weight / jnp.sum(weight, axis=1, keepdims=True)
    values = arrived[:, :, :latent].reshape(pairs, devs, 2 * rows, latent)
    attended = weight[:, 0] * values[:, 0].astype(f32)
    for dev in range(1, devs):
        attended = attended + weight[:, dev] * values[:, dev].astype(f32)
    attended = attended.reshape(pairs * 2 * rows, latent).astype(bf16)

    def head(up, is_own):
        value = jnp.dot(attended, up[...], preferred_element_type=f32)
        value = value.reshape(pairs, 2 * rows, -1)
        low, high = value[:, :rows], value[:, rows:]
        picked = jnp.where(core == (0 if is_own else 1), low, high)
        return picked.reshape(pairs * rows, -1).astype(bf16)

    own, other = head(up_own, True), head(up_other, False)
    weight = out_own.reshape(out_other.shape)
    for copy in copies:
        copy.wait()
    for dev in range(devs):
        columns = slice(dev * share, (dev + 1) * share)
        value = jnp.dot(own, weight[:, columns], preferred_element_type=f32)
        value = value + jnp.dot(other, out_other[:, columns], preferred_element_type=f32)
        part[:, dev] = value.astype(bf16).reshape(pairs, rows, share)


def project(arrived, up_own, up_other, out_own, out_other, pairs, devs):
    rows = arrived.shape[1] // 2
    width = out_other.shape[1]
    return pl.pallas_call(
        project_kernel,
        out_shape=(
            jax.ShapeDtypeStruct((pairs, devs, rows, width // devs), bf16),
            jax.ShapeDtypeStruct((2, pairs, rows, NOTES), f32),
        ),
        in_specs=[VMEM] * 4 + [ANY],
        out_specs=(VMEM, VMEM),
        scratch_shapes=[
            pltpu.VMEM(out_other.shape, bf16),
            pltpu.SemaphoreType.DMA((SLABS,)),
        ],
        compiler_params=pltpu.CompilerParams(vmem_limit_bytes=LIMIT),
        name="project",
    )(arrived, up_own, up_other, pinned(out_own, pltpu.VMEM), pinned(out_other))


def residual_kernel(arrived, hidden, residual, copies):
    share = residual.shape[1]
    start = pl.multiple_of(lax.axis_index("dev") * share, 128)
    total = hidden[:, pl.ds(start, share)].astype(f32)
    total = total + jnp.sum(arrived[...].astype(f32), axis=0)
    residual[...] = total
    copies[...] = jnp.broadcast_to(total.astype(bf16)[None], copies.shape)


def add_up(arrived, hidden):
    return pl.pallas_call(
        residual_kernel,
        out_shape=(
            jax.ShapeDtypeStruct(arrived.shape[1:], f32),
            pltpu.VMEM(arrived.shape, bf16),
        ),
        in_specs=[VMEM, VMEM],
        out_specs=(VMEM, VMEM),
        compiler_params=pltpu.CompilerParams(vmem_limit_bytes=LIMIT),
        name="residual",
    )(arrived, hidden)


def stage_kernel(bands, after, *refs):
    sources, out, arrivals = refs[:-2], refs[-2], refs[-1]
    share = out.shape[1]
    copies = []
    for place, (source, band) in enumerate(bands):
        copies.append(
            pltpu.make_async_copy(
                sources[source].at[pl.ds(band * share, share)], out.at[place], arrivals.at[place]
            )
        )
    for copy in copies:
        copy.start()
    for copy in copies:
        copy.wait()


def stage(after, share, bands, *weights):
    width = weights[0].shape[1]
    return pl.pallas_call(
        functools.partial(stage_kernel, bands),
        out_shape=pltpu.VMEM((len(bands), share, width), bf16),
        in_specs=[ANY] * (len(weights) + 1),
        out_specs=VMEM,
        scratch_shapes=[pltpu.SemaphoreType.DMA((len(bands),))],
        compiler_params=pltpu.CompilerParams(vmem_limit_bytes=4 * 2**20),
        cost_estimate=pl.CostEstimate(
            flops=0, bytes_accessed=4 * len(bands) * share * width, transcendentals=0
        ),
        name="stage",
    )(after, *[pinned(weight) for weight in weights])


def experts_kernel(
    arrived,
    gain,
    coefficients,
    staged,
    gate_own,
    gate_other,
    up_own,
    up_other,
    down_own,
    down_other,
    part,
    first,
    second,
    first_arrivals,
    second_arrivals,
):
    pairs, devs, rows, share = arrived.shape
    width = devs * share
    units = first.shape[2]
    core = lax.axis_index("core")
    copies = []
    for dev in range(devs):
        band = pl.ds(dev * share, share)
        for place, source in enumerate((gate_own, gate_other, up_own, up_other)):
            copies.append(
                pltpu.make_async_copy(
                    source.at[band], first.at[place, band], first_arrivals.at[place, dev]
                )
            )
    for dev in range(devs):
        band = pl.ds(dev * share, share)
        for place, source in enumerate((down_own, down_other)):
            copies.append(
                pltpu.make_async_copy(
                    source.at[:, band], second.at[place, :, band], second_arrivals.at[place, dev]
                )
            )
    copies = copies[STAGED:]
    begun = [copy.start() for copy in copies[:WINDOW]]
    arrived_count = 0

    def receive(until):
        nonlocal arrived_count
        while arrived_count < until - STAGED:
            copies[arrived_count].wait()
            arrived_count += 1
            if len(begun) < len(copies):
                begun.append(copies[len(begun)].start())

    squares = jnp.zeros((pairs * rows, 1), f32)
    sums = [jnp.zeros((pairs * rows, units), f32) for _ in range(4)]
    for dev in range(devs):
        value = arrived[:, dev].astype(f32).reshape(pairs * rows, share)
        squares = squares + jnp.sum(value * value, axis=1, keepdims=True)
        value = (value * gain[dev : dev + 1, :]).astype(bf16)
        receive(4 * dev + 4)
        for place in range(4):
            if 4 * dev + place < STAGED:
                band = staged[4 * dev + place]
            else:
                band = first[place, dev * share : (dev + 1) * share]
            sums[place] = sums[place] + jnp.dot(value, band, preferred_element_type=f32)
    factor = lax.rsqrt(squares * (1.0 / width) + 1e-06)
    activated = []
    for place in range(2):
        gate, up = sums[place] * factor, sums[2 + place] * factor
        mix = jnp.where(core == place, coefficients[0], coefficients[1])
        mix = mix.reshape(pairs * rows, NOTES)[:, :1]
        activated.append((gate / (1.0 + jnp.exp(-gate)) * up * mix).astype(bf16))
    for dev in range(devs):
        receive(4 * devs + 2 * dev + 2)
        columns = slice(dev * share, (dev + 1) * share)
        value = jnp.dot(activated[0], second[0, :, columns], preferred_element_type=f32)
        value = value + jnp.dot(activated[1], second[1, :, columns], preferred_element_type=f32)
        part[:, dev] = value.astype(bf16).reshape(pairs, rows, share)


def experts(arrived, gain, coefficients, staged, *weights):
    pairs, devs, rows, share = arrived.shape
    units = weights[0].shape[1]
    return pl.pallas_call(
        experts_kernel,
        out_shape=jax.ShapeDtypeStruct(arrived.shape, bf16),
        in_specs=[VMEM] * 4 + [ANY] * 6,
        out_specs=VMEM,
        scratch_shapes=[
            pltpu.VMEM((4, devs * share, units), bf16),
            pltpu.VMEM((2, units, devs * share), bf16),
            pltpu.SemaphoreType.DMA((4, devs)),
            pltpu.SemaphoreType.DMA((2, devs)),
        ],
        compiler_params=pltpu.CompilerParams(vmem_limit_bytes=LIMIT),
        name="experts",
    )(
        arrived,
        gain,
        coefficients,
        pinned(staged, pltpu.VMEM),
        *[pinned(weight) for weight in weights],
    )


def finish_kernel(arrived, residual, out):
    out[...] = residual[...] + jnp.sum(arrived[...].astype(f32), axis=0)


def finish(arrived, residual):
    return pl.pallas_call(
        finish_kernel,
        out_shape=jax.ShapeDtypeStruct(residual.shape, f32),
        in_specs=[VMEM, VMEM],
        out_specs=VMEM,
        compiler_params=pltpu.CompilerParams(vmem_limit_bytes=LIMIT),
        name="finish",
    )(arrived, residual)


def on_device(
    hidden,
    queries,
    latent_cache,
    lengths,
    value_up,
    output_weight,
    norm_gain,
    routes,
    route_scores,
    gate_weight,
    up_weight,
    down_weight,
):
    pairs, devs = lax.axis_size("pair"), lax.axis_size("dev")
    chips = pairs * devs
    rows, model_width = hidden.shape
    share = model_width // devs
    latent = value_up.shape[1]
    value_up, gate_weight, up_weight, down_weight = (
        value_up[0],
        gate_weight[0],
        up_weight[0],
        down_weight[0],
    )
    value_other, output_other, gate_other, up_other, down_other = [
        other_core(weight)
        for weight in (value_up, output_weight, gate_weight, up_weight, down_weight)
    ]
    parts = attend(
        lengths,
        routes,
        route_scores,
        jnp.swapaxes(queries, 1, 2),
        jnp.swapaxes(latent_cache, 1, 2),
        latent,
    )
    half = output_weight.shape[0] // 2
    output_own = stage(parts, half, ((0, 0), (0, 1)), output_weight)
    part, coefficients = project(
        exchange(parts), value_up, value_other, output_own, output_other, pairs, devs
    )
    arrived = exchange(part.reshape(chips, rows, share))
    residual, copies = add_up(arrived, hidden)
    bands = tuple((place % 4, place // 4) for place in range(STAGED))
    staged = stage(residual, share, bands, gate_weight, gate_other, up_weight, up_other)
    arrived = exchange(copies).reshape(pairs, devs, rows, share)
    part = experts(
        arrived,
        norm_gain.reshape(devs, share),
        coefficients,
        staged,
        gate_weight,
        gate_other,
        up_weight,
        up_other,
        down_weight,
        down_other,
    )
    return finish(exchange(part.reshape(chips, rows, share)), residual)


def solution(mesh):
    nodes, devs = mesh.devices.shape
    planes = Mesh(mesh.devices.reshape(nodes // 2, 2, devs), ("pair", "core", "dev"))
    node = ("pair", "core")
    both = ("pair", "core", "dev")
    return jax.shard_map(
        on_device,
        mesh=planes,
        in_specs=(
            P(node, None),
            P(node, None, None),
            P(node, "dev", None),
            P(node),
            P(both, None, None),
            P(both, None),
            P(),
            P(node, None),
            P(node, None),
            P(node, None, "dev"),
            P(node, None, "dev"),
            P(node, "dev", None),
        ),
        out_specs=P(node, "dev"),
        check_vma=False,
    )
```

```python
import functools

import jax
import jax.numpy as jnp
from jax import lax
from jax.experimental import pallas as pl
from jax.experimental.pallas import tpu as pltpu
from jax.sharding import Mesh
from jax.sharding import PartitionSpec as P

PLANE = ("pair", "dev")
VMEM = pl.BlockSpec(memory_space=pltpu.VMEM)
SMEM = pl.BlockSpec(memory_space=pltpu.SMEM)
ANY = pl.BlockSpec(memory_space=pl.ANY)
NOTES = 128
SLABS = 2
STAGED = 6
EARLY = 4
CHUNK = 256
LOOK = False
WINDOW = 16
LOG2E = 1.4426950408889634
LIMIT = 40 * 2**20
f32 = jnp.float32
bf16 = jnp.bfloat16


def exchange(blocks):
    return lax.all_to_all(blocks, PLANE, split_axis=0, concat_axis=0, tiled=True)


def other_core(value):
    return lax.ppermute(value, "core", [(0, 1), (1, 0)])


def thirds(value):
    high = value.astype(bf16).astype(f32)
    rest = value - high
    middle = rest.astype(bf16).astype(f32)
    return high, middle, rest - middle


def attend_kernel(
    lengths_in,
    routes_in,
    scores_in,
    query_in,
    cache,
    out,
    held,
    joined,
    query,
    lengths,
    routes,
    route_scores,
    arrivals,
    small_arrivals,
    query_arrivals,
):
    rows, feature, positions = cache.shape
    heads = query.shape[2]
    tiles = joined.shape[0] - 1
    latent = tiles * NOTES
    dev = lax.axis_index("dev")
    dev_count = lax.axis_size("dev")
    small = [
        pltpu.make_async_copy(source, target, small_arrivals.at[place])
        for place, (source, target) in enumerate(
            (
                (lengths_in, lengths),
                (routes_in, routes),
                (scores_in, route_scores),
            )
        )
    ]
    query_copies = [
        pltpu.make_async_copy(query_in.at[row], query.at[row], query_arrivals.at[row])
        for row in range(rows)
    ]
    copies = [
        pltpu.make_async_copy(cache.at[row], held.at[row], arrivals.at[row]) for row in range(rows)
    ]
    for copy in query_copies[:1] + copies[:1] + small + query_copies[1:] + copies[1:]:
        copy.start()
    lane = lax.broadcasted_iota(jnp.int32, (heads, NOTES), 1)
    expert = lax.broadcasted_iota(jnp.int32, (heads, NOTES), 0) // dev_count
    position = lax.broadcasted_iota(jnp.int32, (1, positions), 1)
    scale = feature**-0.5
    for copy in small:
        copy.wait()

    def one_row(row, carry):
        total_score = route_scores[row, 0]
        for k in range(1, routes.shape[1]):
            total_score = total_score + route_scores[row, k]
        named = jnp.zeros((heads, NOTES), f32)
        for k in range(routes.shape[1]):
            named = jnp.where(expert == routes[row, k], route_scores[row, k], named)
        mix = 2.5 * named / total_score
        used = lengths[row] - dev * positions
        pltpu.make_async_copy(query_in.at[row], query.at[row], query_arrivals.at[row]).wait()
        pltpu.make_async_copy(cache.at[row], held.at[row], arrivals.at[row]).wait()

        def store(mean, log_total):
            notes = jnp.zeros((heads, NOTES), f32)
            for place, part in enumerate(thirds(log_total) + thirds(mix)):
                notes = jnp.where(lane == place, part, notes)
            for group in range(heads // 8):
                pair, core = group // 2, group % 2
                target = pl.ds(pair * 64 + core * rows + row, 8, stride=8)
                source = slice(group * 8, group * 8 + 8)
                for tile in range(tiles):
                    joined[tile, target] = mean[source, tile * NOTES : (tile + 1) * NOTES]
                joined[tiles, target] = notes[source]

        @pl.when(used > 0)
        def _():
            scores = lax.dot_general(
                query[row], held[row], (((0,), (0,)), ((), ())), preferred_element_type=f32
            )
            scores = scores + jnp.where(position < used, 0.0, -1e30)
            top = jnp.max(scores, axis=1, keepdims=True)
            total, summed = 0.0, 0.0
            for start in range(0, positions, CHUNK):
                weights = jnp.exp2((scores[:, start : start + CHUNK] - top) * (scale * LOG2E))
                total = total + jnp.sum(weights, axis=1, keepdims=True)
                summed = summed + lax.dot_general(
                    weights.astype(bf16),
                    held[row, :latent, start : start + CHUNK],
                    (((1,), (1,)), ((), ())),
                    preferred_element_type=f32,
                )
            store(summed / total, top * scale + jnp.log(total))

        @pl.when(used <= 0)
        def _():
            store(jnp.zeros((heads, latent), f32), jnp.full((heads, 1), -1e30, f32))

        return carry

    lax.fori_loop(0, rows, one_row, 0)
    for tile in range(tiles + 1):
        columns = slice(tile * NOTES, (tile + 1) * NOTES)
        out[:, :, columns] = joined[tile].astype(bf16).reshape(out.shape[0], out.shape[1], NOTES)


def pinned(value, space=pltpu.HBM):
    return pltpu.with_memory_space_constraint(value, space)


def attend(lengths, routes, route_scores, queries, cache, latent):
    rows, feature, positions = cache.shape
    heads = queries.shape[2]
    return pl.pallas_call(
        attend_kernel,
        out_shape=pltpu.VMEM((heads // 2, 2 * rows, latent + NOTES), bf16),
        in_specs=[ANY] * 5,
        out_specs=VMEM,
        scratch_shapes=[
            pltpu.VMEM((rows, feature, positions), bf16),
            pltpu.VMEM((latent // NOTES + 1, heads * rows, NOTES), f32),
            pltpu.VMEM(queries.shape, bf16),
            pltpu.SMEM(lengths.shape, jnp.int32),
            pltpu.SMEM(routes.shape, jnp.int32),
            pltpu.SMEM(route_scores.shape, f32),
            pltpu.SemaphoreType.DMA((rows,)),
            pltpu.SemaphoreType.DMA((3,)),
            pltpu.SemaphoreType.DMA((rows,)),
        ],
        compiler_params=pltpu.CompilerParams(vmem_limit_bytes=LIMIT),
        cost_estimate=pl.CostEstimate(
            flops=4 * rows * heads * feature * positions,
            bytes_accessed=2 * rows * feature * positions,
            transcendentals=rows * heads * positions,
        ),
        name="attend",
    )(*[pinned(value) for value in (lengths, routes, route_scores, queries, cache)])


def project_kernel(
    arrived, up_own, up_other, out_own, other_in, part, coefficients, out_other, held, arrivals
):
    copies = []
    for cut in range(SLABS):
        band = pl.ds(cut * (out_other.shape[0] // SLABS), out_other.shape[0] // SLABS)
        copies.append(
            pltpu.make_async_copy(other_in.at[band], out_other.at[band], arrivals.at[cut])
        )
        copies[-1].start()
    pairs, devs, rows, share = part.shape
    latent = up_own.shape[0]
    core = lax.axis_index("core")
    notes = arrived[:, :, latent:].astype(f32)
    lane = lax.broadcasted_iota(jnp.int32, notes.shape, 2)
    log_total = jnp.sum(jnp.where(lane < 3, notes, 0.0), axis=2, keepdims=True)
    coefficient = jnp.sum(
        jnp.where((lane >= 3) & (lane < 6), notes, 0.0), axis=2, keepdims=True
    )
    coefficient = coefficient.reshape(pairs, devs, 2 * rows, 1)[:, 0]
    coefficient = jnp.broadcast_to(coefficient, (pairs, 2 * rows, NOTES))
    coefficients[0] = coefficient[:, :rows]
    coefficients[1] = coefficient[:, rows:]
    log_total = log_total.reshape(pairs, devs, 2 * rows, 1)
    weight = jnp.exp(log_total - jnp.max(log_total, axis=1, keepdims=True))
    weight = weight / jnp.sum(weight, axis=1, keepdims=True)
    values = arrived[:, :, :latent].reshape(pairs, devs, 2 * rows, latent)
    attended = weight[:, 0] * values[:, 0].astype(f32)
    for dev in range(1, devs):
        attended = attended + weight[:, dev] * values[:, dev].astype(f32)
    attended = attended.reshape(pairs * 2 * rows, latent).astype(bf16)

    def head(up, is_own):
        value = jnp.dot(attended, up[...], preferred_element_type=f32)
        value = value.reshape(pairs, 2 * rows, -1)
        low, high = value[:, :rows], value[:, rows:]
        picked = jnp.where(core == (0 if is_own else 1), low, high)
        return picked.reshape(pairs * rows, -1).astype(bf16)

    own, other = head(up_own, True), head(up_other, False)
    weight = out_own.reshape(out_other.shape)
    for dev in range(devs):
        columns = slice(dev * share, (dev + 1) * share)
        held[:, columns] = jnp.dot(own, weight[:, columns], preferred_element_type=f32)
    for copy in copies:
        copy.wait()
    for dev in range(devs):
        columns = slice(dev * share, (dev + 1) * share)
        value = held[:, columns] + jnp.dot(
            other, out_other[:, columns], preferred_element_type=f32
        )
        part[:, dev] = value.astype(bf16).reshape(pairs, rows, share)


def project(arrived, up_own, up_other, out_own, out_other, pairs, devs):
    rows = arrived.shape[1] // 2
    width = out_other.shape[1]
    return pl.pallas_call(
        project_kernel,
        out_shape=(
            jax.ShapeDtypeStruct((pairs, devs, rows, width // devs), bf16),
            jax.ShapeDtypeStruct((2, pairs, rows, NOTES), f32),
        ),
        in_specs=[VMEM] * 4 + [ANY],
        out_specs=(VMEM, VMEM),
        scratch_shapes=[
            pltpu.VMEM(out_other.shape, bf16),
            pltpu.VMEM((pairs * rows, width), f32),
            pltpu.SemaphoreType.DMA((SLABS,)),
        ],
        compiler_params=pltpu.CompilerParams(vmem_limit_bytes=LIMIT),
        name="project",
    )(arrived, up_own, up_other, pinned(out_own, pltpu.VMEM), pinned(out_other))


def residual_kernel(arrived, hidden, residual, copies):
    share = residual.shape[1]
    start = pl.multiple_of(lax.axis_index("dev") * share, 128)
    total = hidden[:, pl.ds(start, share)].astype(f32)
    total = total + jnp.sum(arrived[...].astype(f32), axis=0)
    residual[...] = total
    copies[...] = jnp.broadcast_to(total.astype(bf16)[None], copies.shape)


def add_up(arrived, hidden):
    return pl.pallas_call(
        residual_kernel,
        out_shape=(
            jax.ShapeDtypeStruct(arrived.shape[1:], f32),
            pltpu.VMEM(arrived.shape, bf16),
        ),
        in_specs=[VMEM, VMEM],
        out_specs=(VMEM, VMEM),
        compiler_params=pltpu.CompilerParams(vmem_limit_bytes=LIMIT),
        name="residual",
    )(arrived, hidden)


def stage_kernel(bands, after, *refs):
    sources, out, arrivals = refs[:-2], refs[-2], refs[-1]
    share = out.shape[1]
    copies = []
    for place, (source, band) in enumerate(bands):
        copies.append(
            pltpu.make_async_copy(
                sources[source].at[pl.ds(band * share, share)], out.at[place], arrivals.at[place]
            )
        )
    for copy in copies:
        copy.start()
    for copy in copies:
        copy.wait()


def stage(after, share, bands, *weights):
    width = weights[0].shape[1]
    return pl.pallas_call(
        functools.partial(stage_kernel, bands),
        out_shape=pltpu.VMEM((len(bands), share, width), bf16),
        in_specs=[ANY] * (len(weights) + 1),
        out_specs=VMEM,
        scratch_shapes=[pltpu.SemaphoreType.DMA((len(bands),))],
        compiler_params=pltpu.CompilerParams(vmem_limit_bytes=4 * 2**20),
        cost_estimate=pl.CostEstimate(
            flops=0, bytes_accessed=4 * len(bands) * share * width, transcendentals=0
        ),
        name="stage",
    )(after, *[pinned(weight) for weight in weights])


def experts_kernel(
    arrived,
    gain,
    coefficients,
    staged,
    gate_own,
    gate_other,
    up_own,
    up_other,
    down_own,
    down_other,
    part,
    first,
    second,
    first_arrivals,
    second_arrivals,
):
    pairs, devs, rows, share = arrived.shape
    width = devs * share
    units = first.shape[2]
    core = lax.axis_index("core")
    copies = []
    for dev in range(devs):
        band = pl.ds(dev * share, share)
        for place, source in enumerate((gate_own, gate_other, up_own, up_other)):
            copies.append(
                pltpu.make_async_copy(
                    source.at[band], first.at[place, band], first_arrivals.at[place, dev]
                )
            )
    for dev in range(devs):
        band = pl.ds(dev * share, share)
        for place, source in enumerate((down_own, down_other)):
            copies.append(
                pltpu.make_async_copy(
                    source.at[:, band], second.at[place, :, band], second_arrivals.at[place, dev]
                )
            )
    copies = copies[STAGED:]
    begun = [copy.start() for copy in copies[:WINDOW]]
    arrived_count = 0

    def receive(until):
        nonlocal arrived_count
        while arrived_count < until - STAGED:
            copies[arrived_count].wait()
            arrived_count += 1
            if len(begun) < len(copies):
                begun.append(copies[len(begun)].start())

    squares = jnp.zeros((pairs * rows, 1), f32)
    sums = [jnp.zeros((pairs * rows, units), f32) for _ in range(4)]
    for dev in range(devs):
        value = arrived[:, dev].astype(f32).reshape(pairs * rows, share)
        squares = squares + jnp.sum(value * value, axis=1, keepdims=True)
        value = (value * gain[dev : dev + 1, :]).astype(bf16)
        receive(4 * dev + 4)
        for place in range(4):
            if 4 * dev + place < STAGED:
                band = staged[4 * dev + place]
            else:
                band = first[place, dev * share : (dev + 1) * share]
            sums[place] = sums[place] + jnp.dot(value, band, preferred_element_type=f32)
    factor = lax.rsqrt(squares * (1.0 / width) + 1e-06)
    activated = []
    for place in range(2):
        gate, up = sums[place] * factor, sums[2 + place] * factor
        mix = jnp.where(core == place, coefficients[0], coefficients[1])
        mix = mix.reshape(pairs * rows, NOTES)[:, :1]
        activated.append((gate / (1.0 + jnp.exp(-gate)) * up * mix).astype(bf16))
    for dev in range(devs):
        receive(4 * devs + 2 * dev + 2)
        columns = slice(dev * share, (dev + 1) * share)
        value = jnp.dot(activated[0], second[0, :, columns], preferred_element_type=f32)
        value = value + jnp.dot(activated[1], second[1, :, columns], preferred_element_type=f32)
        part[:, dev] = value.astype(bf16).reshape(pairs, rows, share)


def experts(arrived, gain, coefficients, staged, *weights):
    pairs, devs, rows, share = arrived.shape
    units = weights[0].shape[1]
    return pl.pallas_call(
        experts_kernel,
        out_shape=jax.ShapeDtypeStruct(arrived.shape, bf16),
        in_specs=[VMEM] * 4 + [ANY] * 6,
        out_specs=VMEM,
        scratch_shapes=[
            pltpu.VMEM((4, devs * share, units), bf16),
            pltpu.VMEM((2, units, devs * share), bf16),
            pltpu.SemaphoreType.DMA((4, devs)),
            pltpu.SemaphoreType.DMA((2, devs)),
        ],
        compiler_params=pltpu.CompilerParams(vmem_limit_bytes=LIMIT),
        name="experts",
    )(
        arrived,
        gain,
        coefficients,
        pinned(staged, pltpu.VMEM),
        *[pinned(weight) for weight in weights],
    )


def finish_kernel(arrived, residual, out):
    out[...] = residual[...] + jnp.sum(arrived[...].astype(f32), axis=0)


def finish(arrived, residual):
    return pl.pallas_call(
        finish_kernel,
        out_shape=jax.ShapeDtypeStruct(residual.shape, f32),
        in_specs=[VMEM, VMEM],
        out_specs=VMEM,
        compiler_params=pltpu.CompilerParams(vmem_limit_bytes=LIMIT),
        name="finish",
    )(arrived, residual)


def on_device(
    hidden,
    queries,
    latent_cache,
    lengths,
    value_up,
    output_weight,
    norm_gain,
    routes,
    route_scores,
    gate_weight,
    up_weight,
    down_weight,
):
    pairs, devs = lax.axis_size("pair"), lax.axis_size("dev")
    chips = pairs * devs
    rows, model_width = hidden.shape
    share = model_width // devs
    latent = value_up.shape[1]
    value_up, gate_weight, up_weight, down_weight = (
        value_up[0],
        gate_weight[0],
        up_weight[0],
        down_weight[0],
    )
    value_other, output_other, gate_other, up_other, down_other = [
        other_core(weight)
        for weight in (value_up, output_weight, gate_weight, up_weight, down_weight)
    ]
    parts = attend(
        lengths,
        routes,
        route_scores,
        jnp.swapaxes(queries, 1, 2),
        jnp.swapaxes(latent_cache, 1, 2),
        latent,
    )
    half = output_weight.shape[0] // 2
    output_own = stage(parts, half, ((0, 0), (0, 1)), output_weight)
    part, coefficients = project(
        exchange(parts), value_up, value_other, output_own, output_other, pairs, devs
    )
    arrived = exchange(part.reshape(chips, rows, share))
    residual, copies = add_up(arrived, hidden)
    bands = tuple((place % 4, place // 4) for place in range(STAGED))
    staged = stage(residual, share, bands, gate_weight, gate_other, up_weight, up_other)
    arrived = exchange(copies).reshape(pairs, devs, rows, share)
    part = experts(
        arrived,
        norm_gain.reshape(devs, share),
        coefficients,
        staged,
        gate_weight,
        gate_other,
        up_weight,
        up_other,
        down_weight,
        down_other,
    )
    return finish(exchange(part.reshape(chips, rows, share)), residual)


def solution(mesh):
    nodes, devs = mesh.devices.shape
    planes = Mesh(mesh.devices.reshape(nodes // 2, 2, devs), ("pair", "core", "dev"))
    node = ("pair", "core")
    both = ("pair", "core", "dev")
    return jax.shard_map(
        on_device,
        mesh=planes,
        in_specs=(
            P(node, None),
            P(node, None, None),
            P(node, "dev", None),
            P(node),
            P(both, None, None),
            P(both, None),
            P(),
            P(node, None),
            P(node, None),
            P(node, None, "dev"),
            P(node, None, "dev"),
            P(node, "dev", None),
        ),
        out_specs=P(node, "dev"),
        check_vma=False,
    )
```
